256 devices in a mesh: dp: 4 (over x), section: 2 (over core), tensor: 32 (over z, y).
Axes of the slice: x: 4, y: 4, z: 8, core: 2. Of those that a mesh axis runs over, the one named last changes fastest.
Arguments:
- base: bfloat16 [4096, 8192], P('dp', 'tensor'), may hold values from -400 to 400
- deltas: bfloat16 [2, 4096, 8192], P('section', 'dp', 'tensor'), may hold values from -6 to 6
- gain: float32 [8192], P('tensor'), may hold values from 0.5 to 1.5
- lengths: int32 [4], replicated, may hold values from 1 to 1024, 2560 in all
Outputs:
- gram: float32 [2, 8192, 8192], P('section', 'dp', 'tensor')
- cross: float32 [2, 8192, 8192], P('section', 'dp', 'tensor')
The draws below stay inside these ranges and needn't reach their ends.
All inputs are finite; a program needn't handle non-finite values.
Results may differ from the reference program's by a relative error of at most 0.0029.
Values may be sent and summed in bfloat16 or wider, within the bound.
A program may use at most 128 MiB of HBM per device.

```python
import math
import jax
import jax.numpy as jnp
import numpy as np
from jax import lax

D = 8192
TOK_DEV = 1024
TOKENS = 4096
LAYERS = 2
N_DP = 4


def draw_base(key, part):
    key = jax.random.fold_in(key, 11)
    key_values, key_cols, key_rows = jax.random.split(key, 3)
    ramp = 1.0 + 2.0 * jnp.arange(D, dtype=jnp.float32) / D
    columns = jnp.exp(jax.random.uniform(key_cols, (D,), jnp.float32, math.log(0.3), math.log(3.0))) * ramp
    rows = jnp.exp(jax.random.uniform(key_rows, (TOKENS, 1), jnp.float32, 0.0, math.log(10.0)))
    values = jnp.clip(jax.random.normal(key_values, (TOKENS, D), jnp.float32), -4.0, 4.0)
    return (values * rows * columns[None, :]).astype(jnp.bfloat16)


def steps_of(stream_key, extent, cuts, smallest, largest):
    level, own = 1.0, jax.random.fold_in(stream_key, 6)
    for dim, shards_of in cuts:
        steps = jnp.exp(jax.random.uniform(jax.random.fold_in(own, dim), (shards_of,), jnp.float32, smallest / len(cuts), largest / len(cuts)))
        level = level * jnp.repeat(steps, extent[dim] // shards_of).reshape([-1 if axis == dim else 1 for axis in range(len(extent))])
    return level


def profile(number_of, total, bound, slope):
    weights = [(1 << 20) // math.isqrt(rank ** slope) + 1 for rank in range(2, number_of + 1)]
    surplus, counts = total - bound - (number_of - 1), [1] * (number_of - 1)
    while surplus > 0:
        movable = [i for i in range(number_of - 1) if counts[i] < bound]
        pool, budget = sum([weights[i] for i in movable]), surplus
        for i in movable:
            extra = min(bound - counts[i], max(1, budget * weights[i] // pool), surplus)
            counts[i] = counts[i] + extra
            surplus = surplus - extra
    return np.array([bound] + counts)


def ragged_sizes(rng, count, total, bound, slope):
    if count == 2:
        one = jax.random.randint(rng, (), max(1, total - bound), min(bound, total - 1) + 1)
        return jnp.stack([one, total - one])
    sizes = jnp.asarray(profile(count, total, bound, slope), jnp.int32)
    couples = (count - 1) // 2
    source_of, taker = sizes[1:1 + 2 * couples:2], sizes[2:2 + 2 * couples:2]
    slack = jnp.minimum(source_of - 1, bound - taker)
    passed = jax.random.randint(jax.random.fold_in(rng, 1), (couples,), 0, 1 << 20) % (slack + 1)
    sizes = sizes.at[1:1 + 2 * couples:2].set(source_of - passed).at[2:2 + 2 * couples:2].set(taker + passed)
    return sizes[jax.random.permutation(jax.random.fold_in(rng, 2), count)]


def noise(rng, shape, scale, most, pieces=(), held_as=jnp.bfloat16):
    loudness = steps_of(rng, shape, pieces, -0.22, 0.18) if pieces else 1.0
    drawn = jax.random.normal(rng, shape, jnp.float32) * scale * loudness
    return jnp.minimum(jnp.maximum(drawn, -most), most).astype(held_as)


def setup_inputs(seed: int = 0) -> dict:
    key_of = jax.random.split(jax.random.key(seed), 5)
    base = draw_base(jax.random.fold_in(key_of[4], 71), 0)
    deltas = noise(key_of[1], (LAYERS, TOKENS, D), 1.0, 6.0, ((0, 2), (1, 4), (2, 32)))
    gain = jnp.clip(1.0 + 0.1 * jax.random.normal(key_of[2], (D,), jnp.float32), 0.5, 1.5)
    lengths = ragged_sizes(key_of[3], N_DP, N_DP * TOK_DEV * 5 // 8, TOK_DEV, 2).astype(jnp.int32)
    return dict(base=base, deltas=deltas, gain=gain, lengths=lengths)


def normalized(state, live, gain):
    scale = lax.rsqrt(lax.optimization_barrier(jnp.mean(state * state, axis=1, keepdims=True)) + 1e-05)
    return (live * gain[None, :] * state * scale).astype(jnp.bfloat16)

def reference(base, deltas, gain, lengths):
    slots = jnp.arange(TOKENS, dtype=jnp.int32)
    limit = jnp.repeat(lengths, TOK_DEV)
    live = (slots % TOK_DEV < limit).astype(jnp.float32)[:, None]
    count = jnp.sum(lengths).astype(jnp.float32)
    state = base.astype(jnp.float32)
    states = []
    for layer in range(LAYERS):
        state = state + deltas[layer].astype(jnp.float32)
        states.append(state)
    target = normalized(states[-1], live, gain)
    grams = []
    crosses = []
    for layer in range(LAYERS):
        lens = normalized(states[layer], live, gain)
        grams.append(jnp.dot(lens.T, lens, preferred_element_type=jnp.float32) / count)
        crosses.append(jnp.dot(lens.T, target, preferred_element_type=jnp.float32) / count)
    return (jnp.stack(grams), jnp.stack(crosses))
```

```python
import jax
import jax.numpy as jnp
from jax import lax
from jax.experimental import pallas as pl
from jax.experimental.pallas import tpu as pltpu
from jax.sharding import PartitionSpec as P

D = 8192
T = 1024
F = 256
NX, NY, NZ = 4, 4, 8
MESH = pl.DeviceIdType.MESH
LANE = 128


def kernel(
    len_ref, base, delta, gain, out,
    early, turned, zstat, ystat, rows, cols, sbuf, rbuf, fin,
    early_sem, zstat_sem, ystat_sem, z_sem, y_sem, relay_sem, ring_sem, last_sem, local_sem,
):
    f32, bf16 = jnp.float32, jnp.bfloat16
    x, c, t = lax.axis_index("dp"), lax.axis_index("section"), lax.axis_index("tensor")
    z, y = t // NY, t % NY

    def at_x(k):
        return ((x + k) % NX, c, t)

    def at_y(k):
        return (x, c, z * NY + (y + k) % NY)

    def at_z(k):
        return (x, c, ((z + k) % NZ) * NY + y)

    def copy(src, dst, sems, index, device):
        return pltpu.make_async_remote_copy(
            src_ref=src,
            dst_ref=dst,
            send_sem=sems.at[(0, *index)],
            recv_sem=sems.at[(1, *index)],
            device_id=device,
            device_id_type=MESH,
        )

    other = (x, 1 - c, t)

    barrier = pltpu.get_barrier_semaphore()
    peers = [at_z(k) for k in range(1, NZ)] + [at_y(k) for k in range(1, NY)] + [at_x(1), at_x(3), other]
    for peer in peers:
        pl.semaphore_signal(barrier, inc=1, device_id=peer, device_id_type=MESH)
    pl.semaphore_wait(barrier, len(peers))

    early_copy = copy(delta, early, early_sem, (), other)

    @pl.when(c == 0)
    def _():
        early_copy.start()
        early[...] = jnp.zeros_like(early)

    @pl.when(c == 1)
    def _():
        early_copy.wait_recv()

    for k in range(T // LANE):
        part = slice(k * LANE, (k + 1) * LANE)
        state = base[part, :].astype(f32) + early[part, :].astype(f32) + delta[part, :].astype(f32)
        state = state.T
        turned[:, part] = state
        zstat[z, :, part] = jnp.sum(state * state, axis=0, keepdims=True)

    def zstat_copy(k, slot):
        return copy(zstat.at[slot], zstat.at[slot], zstat_sem, (k,), at_z(k))

    def ystat_copy(k, slot):
        return copy(ystat.at[slot], ystat.at[slot], ystat_sem, (k,), at_y(k))

    for k in range(1, NZ):
        zstat_copy(k, z).start()
    for k in range(1, NZ):
        zstat_copy(k, (z + NZ - k) % NZ).wait_recv()
    total = zstat[0]
    for k in range(1, NZ):
        total = total + zstat[k]
    ystat[y] = total
    for k in range(1, NY):
        ystat_copy(k, y).start()
    for k in range(1, NY):
        ystat_copy(k, (y + NY - k) % NY).wait_recv()
    total = ystat[0]
    for k in range(1, NY):
        total = total + ystat[k]
    slots = lax.broadcasted_iota(jnp.int32, (1, T), 1)
    live = jnp.where(slots < len_ref[x], 1.0, 0.0).astype(f32)
    factor = live * lax.rsqrt(total / D + 1e-05)

    gain_down = jnp.broadcast_to(gain[...], (LANE, F)).T
    for k in range(T // LANE):
        part = slice(k * LANE, (k + 1) * LANE)
        lens = gain_down * turned[:, part] * factor[:, part]
        rows[0, :, part] = lens.astype(bf16)
        cols[0, y, part, :] = lens.T.astype(bf16)

    def z_copy(hop, way):
        if hop < 4:
            src = rows.at[0 if hop == 1 else 2 * hop - 3 + way]
            dst = rows.at[2 * hop - 1 + way]
        else:
            half = pl.ds(way * (F // 2), F // 2)
            src, dst = rows.at[5 + way, half], rows.at[7, half]
        return copy(src, dst, z_sem, (2 * (hop - 1) + way,), at_z(1 - 2 * way))

    def y_copy(hop, way, block):
        ref = cols.at[0, block]
        if hop == 2:
            ref = cols.at[0, block, pl.ds(way * (T // 2), T // 2)]
        return copy(ref, ref, y_sem, (2 * (hop - 1) + way,), at_y(1 - 2 * way))

    def relay(k):
        block = (y + (0, 3, 1, 2)[k]) % NY
        return copy(cols.at[0, block], cols.at[1, block], relay_sem, (k,), other)

    def start_relay(k):
        @pl.when(c == 1)
        def _():
            relay(k).start()

    for way in range(2):
        z_copy(1, way).start()
        y_copy(1, way, y).start()
    start_relay(0)
    for way in range(2):
        z_copy(1, way).wait_recv()
        z_copy(2, way).start()
    before, after, across = (y + 3) % NY, (y + 1) % NY, (y + 2) % NY
    y_copy(1, 0, before).wait_recv()
    y_copy(2, 0, before).start()
    start_relay(1)
    y_copy(1, 1, after).wait_recv()
    y_copy(2, 1, after).start()
    start_relay(2)
    for way in range(2):
        y_copy(2, way, across).wait_recv()
    start_relay(3)

    @pl.when(c == 0)
    def _():
        for k in range(4):
            relay(k).wait_recv()

    def place_of(s):
        m = (s + 1) // 2
        zz = (z + NZ + jnp.where(s % 2 == 1, -m, m)) % NZ
        return zz // 2, zz % 2

    def position(dest, way):
        return jnp.where(way == 0, x + NX - dest - 1, dest + NX - 1 - x) % NX

    units = 4 - 2 * c

    def unit_of(way, j):
        r = jnp.where(c == 0, j, 2 * way + j)
        hop = jnp.where(r == 0, 0, jnp.where(r == 3, 2, jnp.where(r == 1, 3, 1)))
        return 4 * way + j, way * (1 - c), hop

    def ring_copy(s, u, way):
        return copy(sbuf.at[s, u], rbuf.at[s, u], ring_sem, (s, u), at_x(jnp.where(way == 0, 1, 3)))

    def last_rows(b, block):
        return pl.ds(pl.multiple_of(b * (NY * F) + block * F, F), F)

    def last_copy(k, b, layer, u, block):
        return copy(fin.at[b, u], out.at[layer, last_rows(b, block)], last_sem, (k, b, layer), at_y(k))

    def local_copy(b, layer, u):
        return pltpu.make_async_copy(fin.at[b, u], out.at[layer, last_rows(b, y)], local_sem.at[b, layer])

    def work(s, p, way):
        dest, b = place_of(s)

        def one(j, carry):
            u, layer, hop = unit_of(way, j)
            acc = jnp.dot(rows[s], cols[layer, (y + hop) % NY], preferred_element_type=f32)
            if p > 0:
                ring_copy(s, u, way).wait_recv()
                acc = acc + rbuf[s, u].astype(f32)
            if p < 3:
                sbuf[s, u] = acc.astype(bf16)
                ring_copy(s, u, way).start()
            else:
                fin[b, u] = acc

                @pl.when(hop == 0)
                def _():
                    local_copy(b, layer, u).start()

                @pl.when(hop != 0)
                def _():
                    last_copy(hop, b, layer, u, y).start()

            return carry

        lax.fori_loop(0, units, one, 0)

    def step(tau, carry):
        for hop in (2, 3, 4):

            @pl.when(tau == hop)
            def _(hop=hop):
                for way in range(2):
                    z_copy(hop, way).wait_recv()
                    if hop < 4:
                        z_copy(hop + 1, way).start()

        for p in range(4):

            def one(k, carry, p=p):
                s = 2 * (tau - p) - 1 + k // 2
                way = k % 2

                @pl.when((s >= 0) & (s < NZ))
                def _():
                    dest, _b = place_of(s)

                    @pl.when(position(dest, way) == p)
                    def _():
                        work(s, p, way)

                return carry

            lax.fori_loop(0, 4, one, 0)
        return carry

    lax.fori_loop(0, 8, step, 0)

    def ending(k, carry):
        b, layer = k % 2, k // 2
        for hop in range(1, NY):
            last_copy(hop, b, layer, 0, (y + NY - hop) % NY).wait_recv()
            last_copy(hop, b, layer, 0, y).wait_send()
        local_copy(b, layer, 0).wait()
        return carry

    lax.fori_loop(0, 2 * (2 - c), ending, 0)

    def sent(k, carry):
        s, way = k // 2, k % 2
        dest, _b = place_of(s)

        @pl.when(position(dest, way) < 3)
        def _():
            def one(j, carry):
                ring_copy(s, 4 * way + j, way).wait_send()
                return carry

            lax.fori_loop(0, units, one, 0)

        return carry

    lax.fori_loop(0, 2 * NZ, sent, 0)
    for k in range(1, NZ):
        zstat_copy(k, z).wait_send()
    for k in range(1, NY):
        ystat_copy(k, y).wait_send()
    for way in range(2):
        for hop in range(1, 5):
            z_copy(hop, way).wait_send()
        y_copy(1, way, y).wait_send()
        y_copy(2, way, (before, after)[way]).wait_send()

    @pl.when(c == 0)
    def _():
        early_copy.wait_send()

    @pl.when(c == 1)
    def _():
        for k in range(4):
            relay(k).wait_send()


def products(lengths, base, delta, gain):
    f32, bf16 = jnp.float32, jnp.bfloat16
    dma = pltpu.SemaphoreType.DMA
    vmem = pl.BlockSpec(memory_space=pltpu.VMEM)
    return pl.pallas_call(
        kernel,
        out_shape=jax.ShapeDtypeStruct((2, 2 * NY * F, F), f32),
        in_specs=[pl.BlockSpec(memory_space=pltpu.SMEM), vmem, vmem, vmem],
        out_specs=pl.BlockSpec(memory_space=pl.ANY),
        scratch_shapes=[
            pltpu.VMEM((T, F), bf16),
            pltpu.VMEM((F, T), f32),
            pltpu.VMEM((NZ, 1, T), f32),
            pltpu.VMEM((NY, 1, T), f32),
            pltpu.VMEM((NZ, F, T), bf16),
            pltpu.VMEM((2, NY, T, F), bf16),
            pltpu.VMEM((NZ, 8, F, F), bf16),
            pltpu.VMEM((NZ, 8, F, F), bf16),
            pltpu.VMEM((2, 8, F, F), f32),
            dma((2,)),
            dma((2, NZ)),
            dma((2, NY)),
            dma((2, 8)),
            dma((2, 4)),
            dma((2, 4)),
            dma((2, NZ, 8)),
            dma((2, NY, 2, 2)),
            dma((2, 2)),
        ],
        compiler_params=pltpu.CompilerParams(
            collective_id=0, has_side_effects=True, vmem_limit_bytes=48 * 1024 * 1024
        ),
        cost_estimate=pl.CostEstimate(flops=8 * 2 * F * T * 2048, bytes_accessed=8 << 20, transcendentals=0),
    )(lengths, base, delta, gain)


def shards(base, deltas, gain, lengths):
    count = jnp.sum(lengths).astype(jnp.float32)
    summed = products(lengths, base, deltas[0], gain[None, :])
    gram = summed[0] / count
    cross = jnp.where(lax.axis_index("section") == 0, summed[1], summed[0]) / count
    return gram[None], cross[None]


def solution(mesh):
    placed = (P("dp", "tensor"), P("section", "dp", "tensor"), P("tensor"), P())
    return jax.shard_map(
        shards,
        mesh=mesh,
        in_specs=placed,
        out_specs=(P("section", "dp", "tensor"), P("section", "dp", "tensor")),
        check_vma=False,
    )
```

```python
import jax
import jax.numpy as jnp
from jax import lax
from jax.experimental import pallas as pl
from jax.experimental.pallas import tpu as pltpu
from jax.sharding import PartitionSpec as P

D = 8192
T = 1024
F = 256
NX, NY, NZ = 4, 4, 8
MESH = pl.DeviceIdType.MESH
LANE = 128
NEAR, FAR, LATE = 2, 4, 3


def kernel(
    len_hbm, base_hbm, delta_hbm, gain_hbm, out,
    len_ref, base, delta, gain, early, turned, zstat, ystat, rows, cols, sbuf, rbuf, fin,
    early_sem, zstat_sem, ystat_sem, z_sem, y_sem, relay_sem, ring_sem, last_sem, local_sem, in_sem,
):
    f32, bf16 = jnp.float32, jnp.bfloat16
    x, c, t = lax.axis_index("dp"), lax.axis_index("section"), lax.axis_index("tensor")
    z, y = t // NY, t % NY

    def at_x(k):
        return ((x + k) % NX, c, t)

    def at_y(k):
        return (x, c, z * NY + (y + k) % NY)

    def at_z(k):
        return (x, c, ((z + k) % NZ) * NY + y)

    def copy(src, dst, sems, index, device):
        return pltpu.make_async_remote_copy(
            src_ref=src,
            dst_ref=dst,
            send_sem=sems.at[(0, *index)],
            recv_sem=sems.at[(1, *index)],
            device_id=device,
            device_id_type=MESH,
        )

    other = (x, 1 - c, t)

    fetches = [
        pltpu.make_async_copy(src, dst, in_sem.at[k])
        for k, (src, dst) in enumerate(((base_hbm, base), (delta_hbm, delta), (gain_hbm, gain), (len_hbm, len_ref)))
    ]
    for fetch in fetches:
        fetch.start()

    barrier = pltpu.get_barrier_semaphore()
    peers = [at_z(k) for k in range(1, NZ)] + [at_y(k) for k in range(1, NY)] + [at_x(1), at_x(3), other]
    for peer in peers:
        pl.semaphore_signal(barrier, inc=1, device_id=peer, device_id_type=MESH)
    pl.semaphore_wait(barrier, len(peers))

    early_copy = copy(delta_hbm, early, early_sem, (), other)

    @pl.when(c == 0)
    def _():
        early_copy.start()
        early[...] = jnp.zeros_like(early)

    for fetch in fetches:
        fetch.wait()

    @pl.when(c == 1)
    def _():
        early_copy.wait_recv()

    for k in range(T // LANE):
        part = slice(k * LANE, (k + 1) * LANE)
        state = base[part, :].astype(f32) + early[part, :].astype(f32) + delta[part, :].astype(f32)
        state = state.T
        turned[:, part] = state
        zstat[z, :, part] = jnp.sum(state * state, axis=0, keepdims=True)

    def zstat_copy(k, slot):
        return copy(zstat.at[slot], zstat.at[slot], zstat_sem, (k,), at_z(k))

    def ystat_copy(k, slot):
        return copy(ystat.at[slot], ystat.at[slot], ystat_sem, (k,), at_y(k))

    for k in range(1, NZ):
        zstat_copy(k, z).start()
    for k in range(1, NZ):
        zstat_copy(k, (z + NZ - k) % NZ).wait_recv()
    total = zstat[0]
    for k in range(1, NZ):
        total = total + zstat[k]
    ystat[y] = total
    for k in range(1, NY):
        ystat_copy(k, y).start()
    for k in range(1, NY):
        ystat_copy(k, (y + NY - k) % NY).wait_recv()
    total = ystat[0]
    for k in range(1, NY):
        total = total + ystat[k]
    slots = lax.broadcasted_iota(jnp.int32, (1, T), 1)
    live = jnp.where(slots < len_ref[x], 1.0, 0.0).astype(f32)
    count = (len_ref[0] + len_ref[1] + len_ref[2] + len_ref[3]).astype(f32)
    factor = live * lax.rsqrt(total / D + 1e-05)

    gain_down = jnp.broadcast_to(gain[...], (LANE, F)).T
    for k in range(T // LANE):
        part = slice(k * LANE, (k + 1) * LANE)
        lens = gain_down * turned[:, part] * factor[:, part]
        rows[0, :, part] = lens.astype(bf16)
        cols[0, y, part, :] = lens.T.astype(bf16)

    def z_copy(hop, way):
        if hop < 4:
            src = rows.at[0 if hop == 1 else 2 * hop - 3 + way]
            dst = rows.at[2 * hop - 1 + way]
        else:
            half = pl.ds(way * (F // 2), F // 2)
            src, dst = rows.at[5 + way, half], rows.at[7, half]
        return copy(src, dst, z_sem, (2 * (hop - 1) + way,), at_z(1 - 2 * way))

    def y_copy(hop, way, block):
        ref = cols.at[0, block]
        if hop == 2:
            ref = cols.at[0, block, pl.ds(way * (T // 2), T // 2)]
        return copy(ref, ref, y_sem, (2 * (hop - 1) + way,), at_y(1 - 2 * way))

    def relay(k):
        block = (y + (0, 3, 1, 2)[k]) % NY
        return copy(cols.at[0, block], cols.at[1, block], relay_sem, (k,), other)

    def start_relay(k):
        @pl.when(c == 1)
        def _():
            relay(k).start()

    before, after, across = (y + 3) % NY, (y + 1) % NY, (y + 2) % NY

    def rows_out():
        for way in range(2):
            z_copy(1, way).start()

    for way in range(2):
        y_copy(1, way, y).start()
    start_relay(0)
    pl.when(c == 0)(rows_out)

    def rows_in(hop):
        for way in range(2):
            z_copy(hop, way).wait_recv()
            if hop < 4:
                z_copy(hop + 1, way).start()

    def columns_near():
        y_copy(1, 0, before).wait_recv()
        y_copy(2, 0, before).start()
        y_copy(1, 1, after).wait_recv()
        y_copy(2, 1, after).start()
        start_relay(1)
        start_relay(2)
        pl.when(c == 1)(rows_out)

    def columns_far():
        for way in range(2):
            y_copy(2, way, across).wait_recv()
        start_relay(3)

    def relayed(*ks):
        @pl.when(c == 0)
        def _():
            for k in ks:
                relay(k).wait_recv()

    def place_of(s):
        m = (s + 1) // 2
        zz = (z + NZ + jnp.where(s % 2 == 1, -m, m)) % NZ
        return zz // 2, zz % 2

    def position(dest, way):
        return jnp.where(way == 0, x + NX - dest - 1, dest + NX - 1 - x) % NX

    units = 4 - 2 * c

    def unit_of(way, j):
        r = jnp.where(c == 0, j, 2 * way + j)
        hop = jnp.where(r == 0, 0, jnp.where(r == 3, 2, jnp.where(r == 1, 3, 1)))
        return 4 * way + j, way * (1 - c), hop

    def ring_copy(s, u, way):
        return copy(sbuf.at[s, u], rbuf.at[s, u], ring_sem, (s, u), at_x(jnp.where(way == 0, 1, 3)))

    def last_rows(b, block):
        return pl.ds(pl.multiple_of(b * (NY * F) + block * F, F), F)

    def last_copy(k, b, layer, u, block):
        return copy(fin.at[b, u], out.at[layer, last_rows(b, block)], last_sem, (k, b, layer), at_y(k))

    def local_copy(b, layer, u):
        return pltpu.make_async_copy(fin.at[b, u], out.at[layer, last_rows(b, y)], local_sem.at[b, layer])

    def work(s, p, way, first, last):
        dest, b = place_of(s)

        def one(r, carry):
            j = jnp.where(c == 0, r, r - 2 * way)
            u, layer, hop = unit_of(way, j)
            acc = jnp.dot(rows[s], cols[layer, (y + hop) % NY], preferred_element_type=f32)
            if p > 0:
                ring_copy(s, u, way).wait_recv()
                acc = acc + rbuf[s, u].astype(f32)
            if p < 3:
                sbuf[s, u] = acc.astype(bf16)
                ring_copy(s, u, way).start()
            else:
                fin[b, u] = (acc / count).astype(bf16)

                @pl.when(hop == 0)
                def _():
                    local_copy(b, layer, u).start()

                @pl.when(hop != 0)
                def _():
                    last_copy(hop, b, layer, u, y).start()

            return carry

        lax.fori_loop(first, last, one, 0)

    def columns_by(a):
        return jnp.where(a < NEAR, 1, jnp.where(a < FAR, 3, 4))

    def rows_at(s):
        m = (s + 1) // 2
        return m + jnp.where((c == 1) & (m > 0), LATE, 0)

    def step(tau, carry):
        for hop in range(1, 5):

            @pl.when(tau == rows_at(2 * hop - 1))
            def _(hop=hop):
                rows_in(hop)

        @pl.when(tau == NEAR)
        def _():
            columns_near()
            relayed(1, 2)

        @pl.when(tau == FAR)
        def _():
            columns_far()
            relayed(3)

        for p in range(4):
            a = tau - p
            m = jnp.maximum(jnp.minimum(jnp.where(c == 1, a - LATE, a), 4), 0)
            s_to = jnp.minimum(2 * m + 1, NZ)
            s_from = jnp.where((a == NEAR) | (a == FAR), 0, jnp.maximum(2 * m - 1, 0))
            upto, already = columns_by(a), jnp.where(a == 0, 0, columns_by(a - 1))

            def one(k, carry, p=p, a=a, upto=upto, already=already):
                s, way = k // 2, k % 2
                dest, _b = place_of(s)

                @pl.when((a >= 0) & (a <= 4 + LATE) & (position(dest, way) == p))
                def _():
                    first = jnp.where(rows_at(s) == a, 0, already)
                    low, high = jnp.where(c == 0, 0, 2 * way), jnp.where(c == 0, 4, 2 * way + 2)
                    work(s, p, way, jnp.maximum(first, low), jnp.minimum(upto, high))

                return carry

            lax.fori_loop(2 * s_from, 2 * s_to, one, 0)
        return carry

    relayed(0)
    lax.fori_loop(0, 4 + LATE + 4, step, 0)

    def ending(k, carry):
        b, layer = k % 2, k // 2
        for hop in range(1, NY):
            last_copy(hop, b, layer, 0, (y + NY - hop) % NY).wait_recv()
            last_copy(hop, b, layer, 0, y).wait_send()
        local_copy(b, layer, 0).wait()
        return carry

    lax.fori_loop(0, 2 * (2 - c), ending, 0)

    def sent(k, carry):
        s, way = k // 2, k % 2
        dest, _b = place_of(s)

        @pl.when(position(dest, way) < 3)
        def _():
            def one(j, carry):
                ring_copy(s, 4 * way + j, way).wait_send()
                return carry

            lax.fori_loop(0, units, one, 0)

        return carry

    lax.fori_loop(0, 2 * NZ, sent, 0)
    for k in range(1, NZ):
        zstat_copy(k, z).wait_send()
    for k in range(1, NY):
        ystat_copy(k, y).wait_send()
    for way in range(2):
        for hop in range(1, 5):
            z_copy(hop, way).wait_send()
        y_copy(1, way, y).wait_send()
        y_copy(2, way, (before, after)[way]).wait_send()

    @pl.when(c == 0)
    def _():
        early_copy.wait_send()

    @pl.when(c == 1)
    def _():
        for k in range(4):
            relay(k).wait_send()


def products(lengths, base, delta, gain):
    f32, bf16 = jnp.float32, jnp.bfloat16
    dma = pltpu.SemaphoreType.DMA
    return pl.pallas_call(
        kernel,
        out_shape=jax.ShapeDtypeStruct((2, 2 * NY * F, F), bf16),
        in_specs=[pl.BlockSpec(memory_space=pl.ANY)] * 4,
        out_specs=pl.BlockSpec(memory_space=pl.ANY),
        scratch_shapes=[
            pltpu.SMEM((NX,), jnp.int32),
            pltpu.VMEM((T, F), bf16),
            pltpu.VMEM((T, F), bf16),
            pltpu.VMEM((1, F), f32),
            pltpu.VMEM((T, F), bf16),
            pltpu.VMEM((F, T), f32),
            pltpu.VMEM((NZ, 1, T), f32),
            pltpu.VMEM((NY, 1, T), f32),
            pltpu.VMEM((NZ, F, T), bf16),
            pltpu.VMEM((2, NY, T, F), bf16),
            pltpu.VMEM((NZ, 8, F, F), bf16),
            pltpu.VMEM((NZ, 8, F, F), bf16),
            pltpu.VMEM((2, 8, F, F), bf16),
            dma((2,)),
            dma((2, NZ)),
            dma((2, NY)),
            dma((2, 8)),
            dma((2, 4)),
            dma((2, 4)),
            dma((2, NZ, 8)),
            dma((2, NY, 2, 2)),
            dma((2, 2)),
            dma((4,)),
        ],
        compiler_params=pltpu.CompilerParams(
            collective_id=0, has_side_effects=True, vmem_limit_bytes=48 * 1024 * 1024
        ),
        cost_estimate=pl.CostEstimate(flops=8 * 2 * F * T * 2048, bytes_accessed=8 << 20, transcendentals=0),
    )(lengths, base, delta, gain)


def shards(base, deltas, gain, lengths):
    summed = products(lengths, base, deltas[0], gain[None, :]).astype(jnp.float32)
    gram = summed[0]
    cross = jnp.where(lax.axis_index("section") == 0, summed[1], summed[0])
    return gram[None], cross[None]


def solution(mesh):
    placed = (P("dp", "tensor"), P("section", "dp", "tensor"), P("tensor"), P())
    return jax.shard_map(
        shards,
        mesh=mesh,
        in_specs=placed,
        out_specs=(P("section", "dp", "tensor"), P("section", "dp", "tensor")),
        check_vma=False,
    )
```

```python
import jax
import jax.numpy as jnp
from jax import lax
from jax.experimental import pallas as pl
from jax.experimental.pallas import tpu as pltpu
from jax.sharding import PartitionSpec as P

D = 8192
T = 1024
F = 256
NX, NY, NZ = 4, 4, 8
MESH = pl.DeviceIdType.MESH
LANE = 128
ROWS = ((0, 2, 3, 6, 7), (0, 2, 6, 8, 9))
COLUMNS = ((6, 7), (3, 6))
LAGS = ((0, 1, 2, 4), (0, 1, 2, 4))
START = 0
STEPS = 1 + max(max(max(ROWS[k]), max(COLUMNS[k])) + LAGS[k][3] for k in range(2))


def kernel(
    len_hbm, base_hbm, delta_hbm, gain_hbm, out,
    len_ref, base, delta, gain, early, turned, zstat, ystat, rows, cols, sbuf, rbuf, fin, own,
    early_sem, zstat_sem, ystat_sem, z_sem, y_sem, relay_sem, ring_sem, last_sem, local_sem, in_sem,
):
    f32, bf16 = jnp.float32, jnp.bfloat16
    x, c, t = lax.axis_index("dp"), lax.axis_index("section"), lax.axis_index("tensor")
    z, y = t // NY, t % NY

    def at_x(k):
        return ((x + k) % NX, c, t)

    def at_y(k):
        return (x, c, z * NY + (y + k) % NY)

    def at_z(k):
        return (x, c, ((z + k) % NZ) * NY + y)

    def copy(src, dst, sems, index, device):
        return pltpu.make_async_remote_copy(
            src_ref=src,
            dst_ref=dst,
            send_sem=sems.at[(0, *index)],
            recv_sem=sems.at[(1, *index)],
            device_id=device,
            device_id_type=MESH,
        )

    other = (x, 1 - c, t)

    fetches = [
        pltpu.make_async_copy(src, dst, in_sem.at[k])
        for k, (src, dst) in enumerate(((base_hbm, base), (delta_hbm, delta), (gain_hbm, gain), (len_hbm, len_ref)))
    ]
    for fetch in fetches:
        fetch.start()

    barrier = pltpu.get_barrier_semaphore()
    peers = [at_z(k) for k in range(1, NZ)] + [at_y(k) for k in range(1, NY)] + [at_x(1), at_x(3), other]
    for peer in peers:
        pl.semaphore_signal(barrier, inc=1, device_id=peer, device_id_type=MESH)
    pl.semaphore_wait(barrier, len(peers))

    early_copy = copy(delta_hbm, early, early_sem, (), other)

    @pl.when(c == 0)
    def _():
        early_copy.start()
        early[...] = jnp.zeros_like(early)

    for fetch in fetches:
        fetch.wait()

    @pl.when(c == 1)
    def _():
        early_copy.wait_recv()

    for k in range(T // LANE):
        part = slice(k * LANE, (k + 1) * LANE)
        state = base[part, :].astype(f32) + early[part, :].astype(f32) + delta[part, :].astype(f32)
        state = state.T
        turned[:, part] = state
        zstat[z, :, part] = jnp.sum(state * state, axis=0, keepdims=True)

    def zstat_copy(k, slot):
        return copy(zstat.at[slot], zstat.at[slot], zstat_sem, (k,), at_z(k))

    def ystat_copy(k, slot):
        return copy(ystat.at[slot], ystat.at[slot], ystat_sem, (k,), at_y(k))

    for k in range(1, NZ):
        zstat_copy(k, z).start()
    for k in range(1, NZ):
        zstat_copy(k, (z + NZ - k) % NZ).wait_recv()
    total = zstat[0]
    for k in range(1, NZ):
        total = total + zstat[k]
    ystat[y] = total
    for k in range(1, NY):
        ystat_copy(k, y).start()
    for k in range(1, NY):
        ystat_copy(k, (y + NY - k) % NY).wait_recv()
    total = ystat[0]
    for k in range(1, NY):
        total = total + ystat[k]
    slots = lax.broadcasted_iota(jnp.int32, (1, T), 1)
    live = jnp.where(slots < len_ref[x], 1.0, 0.0).astype(f32)
    count = (len_ref[0] + len_ref[1] + len_ref[2] + len_ref[3]).astype(f32)
    factor = live * lax.rsqrt(total / D + 1e-05)

    gain_down = jnp.broadcast_to(gain[...], (LANE, F)).T
    for k in range(T // LANE):
        part = slice(k * LANE, (k + 1) * LANE)
        lens = gain_down * turned[:, part] * factor[:, part]
        rows[0, :, part] = lens.astype(bf16)
        cols[0, y, part, :] = lens.T.astype(bf16)

    def z_copy(hop, way):
        if hop < 4:
            src = rows.at[0 if hop == 1 else 2 * hop - 3 + way]
            dst = rows.at[2 * hop - 1 + way]
        else:
            half = pl.ds(way * (F // 2), F // 2)
            src, dst = rows.at[5 + way, half], rows.at[7, half]
        return copy(src, dst, z_sem, (2 * (hop - 1) + way,), at_z(1 - 2 * way))

    def y_copy(hop, way, block):
        ref = cols.at[0, block]
        if hop == 2:
            ref = cols.at[0, block, pl.ds(way * (T // 2), T // 2)]
        return copy(ref, ref, y_sem, (2 * (hop - 1) + way,), at_y(1 - 2 * way))

    def relay(k):
        block = (y + (0, 3, 1, 2)[k]) % NY
        return copy(cols.at[0, block], cols.at[1, block], relay_sem, (k,), other)

    def start_relay(k):
        @pl.when(c == 1)
        def _():
            relay(k).start()

    before, after, across = (y + 3) % NY, (y + 1) % NY, (y + 2) % NY

    def rows_out():
        for way in range(2):
            z_copy(1, way).start()

    for way in range(2):
        y_copy(1, way, y).start()
    start_relay(0)
    pl.when(c == 0)(rows_out)

    def rows_in(hop):
        for way in range(2):
            z_copy(hop, way).wait_recv()
            if hop < 4:
                z_copy(hop + 1, way).start()

    def columns_near():
        y_copy(1, 0, before).wait_recv()
        y_copy(2, 0, before).start()
        y_copy(1, 1, after).wait_recv()
        y_copy(2, 1, after).start()
        start_relay(1)
        start_relay(2)

    def columns_far():
        for way in range(2):
            y_copy(2, way, across).wait_recv()
        start_relay(3)

    def relayed(*ks):
        @pl.when(c == 0)
        def _():
            for k in ks:
                relay(k).wait_recv()

    def place_of(s):
        m = (s + 1) // 2
        zz = (z + NZ + jnp.where(s % 2 == 1, -m, m)) % NZ
        return zz // 2, zz % 2

    def position(dest, way):
        return jnp.where(way == 0, x + NX - dest - 1, dest + NX - 1 - x) % NX

    units = 4 - 2 * c

    def unit_of(way, j):
        r = jnp.where(c == 0, j, 2 * way + j)
        hop = jnp.where(r == 0, 0, jnp.where(r == 3, 2, jnp.where(r == 1, 3, 1)))
        return 4 * way + j, way * (1 - c), hop

    def ring_copy(s, u, way):
        return copy(sbuf.at[s, u], rbuf.at[s, u], ring_sem, (s, u), at_x(jnp.where(way == 0, 1, 3)))

    def last_rows(b, block):
        return pl.ds(pl.multiple_of(b * (NY * F) + block * F, F), F)

    def last_copy(k, b, layer, u, block):
        return copy(fin.at[b, u], out.at[layer, last_rows(b, block)], last_sem, (k, b, layer), at_y(k))

    def local_copy(b, layer, u):
        return pltpu.make_async_copy(fin.at[b, u], out.at[layer, last_rows(b, y)], local_sem.at[b, layer])

    def multiply(s, starts, way, first, last):
        def one(r, carry):
            u, layer, hop = unit_of(way, jnp.where(c == 0, r, r - 2 * way))
            acc = jnp.dot(rows[s], cols[layer, (y + hop) % NY], preferred_element_type=f32)
            if starts:
                sbuf[s, u] = acc.astype(bf16)
                ring_copy(s, u, way).start()
            else:
                own[s, u] = acc
            return carry

        lax.fori_loop(first, last, one, 0)

    def add(s, p, way, first, last):
        _dest, b = place_of(s)

        def one(r, carry):
            u, layer, hop = unit_of(way, jnp.where(c == 0, r, r - 2 * way))
            ring_copy(s, u, way).wait_recv()
            acc = own[s, u] + rbuf[s, u].astype(f32)
            if p < 3:
                sbuf[s, u] = acc.astype(bf16)
                ring_copy(s, u, way).start()
            else:
                fin[b, u] = (acc / count).astype(bf16)

                @pl.when(hop == 0)
                def _():
                    local_copy(b, layer, u).start()

                @pl.when(hop != 0)
                def _():
                    last_copy(hop, b, layer, u, y).start()

            return carry

        lax.fori_loop(first, last, one, 0)

    def mine(pair):
        return jnp.where(c == 0, pair[0], pair[1])

    rows_step = [mine([way[g] for way in ROWS]) for g in range(5)]
    near, far = [mine([way[k] for way in COLUMNS]) for k in range(2)]

    def columns_by(a):
        return jnp.where(a < near, 1, jnp.where(a < far, 3, 4))

    def rows_at(s):
        m = (s + 1) // 2
        at = rows_step[0]
        for g in range(1, 5):
            at = jnp.where(m == g, rows_step[g], at)
        return at

    def step(tau, carry):
        @pl.when((c == 1) & (tau == START))
        def _():
            rows_out()

        @pl.when(tau == near)
        def _():
            columns_near()
            relayed(1, 2)

        @pl.when(tau == far)
        def _():
            columns_far()
            relayed(3)

        for hop in range(1, 5):

            @pl.when(tau == rows_step[hop])
            def _(hop=hop):
                rows_in(hop)

        for turn in range(5):
            p = turn % 4
            a = tau - mine([way[p] for way in LAGS])
            before_a = sum(jnp.where(at < a, 1, 0) for at in rows_step)
            by_a = sum(jnp.where(at <= a, 1, 0) for at in rows_step)
            s_from = jnp.where((a == near) | (a == far), 0, jnp.maximum(2 * before_a - 1, 0))
            s_to = jnp.minimum(jnp.maximum(2 * by_a - 1, 0), NZ)
            upto, already = columns_by(a), columns_by(a - 1)

            def one(k, carry, turn=turn, p=p, a=a, upto=upto, already=already):
                s, way = k // 2, k % 2
                at = position(place_of(s)[0], way)

                @pl.when(at > 0 if turn == 4 else at == p)
                def _():
                    first = jnp.where(rows_at(s) == a, 0, already)
                    low, high = jnp.where(c == 0, 0, 2 * way), jnp.where(c == 0, 4, 2 * way + 2)
                    first, last = jnp.maximum(first, low), jnp.minimum(upto, high)
                    if p == 0:
                        multiply(s, turn == 0, way, first, last)
                    else:
                        add(s, p, way, first, last)

                return carry

            lax.fori_loop(2 * s_from, 2 * s_to, one, 0)
        return carry

    relayed(0)
    lax.fori_loop(0, STEPS, step, 0)

    def ending(k, carry):
        b, layer = k % 2, k // 2
        for hop in range(1, NY):
            last_copy(hop, b, layer, 0, (y + NY - hop) % NY).wait_recv()
            last_copy(hop, b, layer, 0, y).wait_send()
        local_copy(b, layer, 0).wait()
        return carry

    lax.fori_loop(0, 2 * (2 - c), ending, 0)

    def sent(k, carry):
        s, way = k // 2, k % 2
        dest, _b = place_of(s)

        @pl.when(position(dest, way) < 3)
        def _():
            def one(j, carry):
                ring_copy(s, 4 * way + j, way).wait_send()
                return carry

            lax.fori_loop(0, units, one, 0)

        return carry

    lax.fori_loop(0, 2 * NZ, sent, 0)
    for k in range(1, NZ):
        zstat_copy(k, z).wait_send()
    for k in range(1, NY):
        ystat_copy(k, y).wait_send()
    for way in range(2):
        for hop in range(1, 5):
            z_copy(hop, way).wait_send()
        y_copy(1, way, y).wait_send()
        y_copy(2, way, (before, after)[way]).wait_send()

    @pl.when(c == 0)
    def _():
        early_copy.wait_send()

    @pl.when(c == 1)
    def _():
        for k in range(4):
            relay(k).wait_send()


def products(lengths, base, delta, gain):
    f32, bf16 = jnp.float32, jnp.bfloat16
    dma = pltpu.SemaphoreType.DMA
    return pl.pallas_call(
        kernel,
        out_shape=jax.ShapeDtypeStruct((2, 2 * NY * F, F), bf16),
        in_specs=[pl.BlockSpec(memory_space=pl.ANY)] * 4,
        out_specs=pl.BlockSpec(memory_space=pl.ANY),
        scratch_shapes=[
            pltpu.SMEM((NX,), jnp.int32),
            pltpu.VMEM((T, F), bf16),
            pltpu.VMEM((T, F), bf16),
            pltpu.VMEM((1, F), f32),
            pltpu.VMEM((T, F), bf16),
            pltpu.VMEM((F, T), f32),
            pltpu.VMEM((NZ, 1, T), f32),
            pltpu.VMEM((NY, 1, T), f32),
            pltpu.VMEM((NZ, F, T), bf16),
            pltpu.VMEM((2, NY, T, F), bf16),
            pltpu.VMEM((NZ, 8, F, F), bf16),
            pltpu.VMEM((NZ, 8, F, F), bf16),
            pltpu.VMEM((2, 8, F, F), bf16),
            pltpu.VMEM((NZ, 8, F, F), f32),
            dma((2,)),
            dma((2, NZ)),
            dma((2, NY)),
            dma((2, 8)),
            dma((2, 4)),
            dma((2, 4)),
            dma((2, NZ, 8)),
            dma((2, NY, 2, 2)),
            dma((2, 2)),
            dma((4,)),
        ],
        compiler_params=pltpu.CompilerParams(
            collective_id=0, has_side_effects=True, vmem_limit_bytes=62 * 1024 * 1024
        ),
        cost_estimate=pl.CostEstimate(flops=8 * 2 * F * T * 2048, bytes_accessed=8 << 20, transcendentals=0),
    )(lengths, base, delta, gain)


def shards(base, deltas, gain, lengths):
    summed = products(lengths, base, deltas[0], gain[None, :]).astype(jnp.float32)
    gram = summed[0]
    cross = jnp.where(lax.axis_index("section") == 0, summed[1], summed[0])
    return gram[None], cross[None]


def solution(mesh):
    placed = (P("dp", "tensor"), P("section", "dp", "tensor"), P("tensor"), P())
    return jax.shard_map(
        shards,
        mesh=mesh,
        in_specs=placed,
        out_specs=(P("section", "dp", "tensor"), P("section", "dp", "tensor")),
        check_vma=False,
    )
```

```python
import jax
import jax.numpy as jnp
from jax import lax
from jax.experimental import pallas as pl
from jax.experimental.pallas import tpu as pltpu
from jax.sharding import PartitionSpec as P

D = 8192
T = 1024
F = 256
NX, NY, NZ = 4, 4, 8
MESH = pl.DeviceIdType.MESH
LANE = 128
ROWS = ((0, 2, 3, 6, 7), (0, 2, 6, 8, 9))
COLUMNS = ((6, 7), (3, 6))
LAGS = ((0, 1, 2, 4), (0, 1, 2, 4))
START = 0
STEPS = 1 + max(max(max(ROWS[k]), max(COLUMNS[k])) + LAGS[k][3] for k in range(2))


def kernel(
    len_hbm, base_hbm, delta_hbm, gain_hbm, out,
    len_ref, base, delta, gain, early, turned, zstat, ystat, rows, cols, sbuf, rbuf, fin, own,
    early_sem, zstat_sem, ystat_sem, z_sem, y_sem, relay_sem, ring_sem, last_sem, local_sem, in_sem,
):
    f32, bf16 = jnp.float32, jnp.bfloat16
    x, c, t = lax.axis_index("dp"), lax.axis_index("section"), lax.axis_index("tensor")
    z, y = t // NY, t % NY

    def at_x(k):
        return ((x + k) % NX, c, t)

    def at_y(k):
        return (x, c, z * NY + (y + k) % NY)

    def at_z(k):
        return (x, c, ((z + k) % NZ) * NY + y)

    def copy(src, dst, sems, index, device):
        return pltpu.make_async_remote_copy(
            src_ref=src,
            dst_ref=dst,
            send_sem=sems.at[(0, *index)],
            recv_sem=sems.at[(1, *index)],
            device_id=device,
            device_id_type=MESH,
        )

    other = (x, 1 - c, t)

    fetches = [
        pltpu.make_async_copy(src, dst, in_sem.at[k])
        for k, (src, dst) in enumerate(((base_hbm, base), (delta_hbm, delta), (gain_hbm, gain), (len_hbm, len_ref)))
    ]
    for fetch in fetches:
        fetch.start()

    barrier = pltpu.get_barrier_semaphore()
    peers = [at_z(k) for k in range(1, NZ)] + [at_y(k) for k in range(1, NY)] + [at_x(1), at_x(3), other]
    for peer in peers:
        pl.semaphore_signal(barrier, inc=1, device_id=peer, device_id_type=MESH)
    pl.semaphore_wait(barrier, len(peers))

    early_copy = copy(delta_hbm, early, early_sem, (), other)

    @pl.when(c == 0)
    def _():
        early_copy.start()
        early[...] = jnp.zeros_like(early)

    for fetch in fetches:
        fetch.wait()

    @pl.when(c == 1)
    def _():
        early_copy.wait_recv()

    for k in range(T // LANE):
        part = slice(k * LANE, (k + 1) * LANE)
        state = base[part, :].astype(f32) + early[part, :].astype(f32) + delta[part, :].astype(f32)
        state = state.T
        turned[:, part] = state
        zstat[z, :, part] = jnp.sum(state * state, axis=0, keepdims=True)

    def zstat_copy(k, slot):
        return copy(zstat.at[slot], zstat.at[slot], zstat_sem, (k,), at_z(k))

    def ystat_copy(k, slot):
        return copy(ystat.at[slot], ystat.at[slot], ystat_sem, (k,), at_y(k))

    for k in range(1, NZ):
        zstat_copy(k, z).start()
    for k in range(1, NZ):
        zstat_copy(k, (z + NZ - k) % NZ).wait_recv()
    total = zstat[0]
    for k in range(1, NZ):
        total = total + zstat[k]
    ystat[y] = total
    for k in range(1, NY):
        ystat_copy(k, y).start()
    for k in range(1, NY):
        ystat_copy(k, (y + NY - k) % NY).wait_recv()
    total = ystat[0]
    for k in range(1, NY):
        total = total + ystat[k]
    slots = lax.broadcasted_iota(jnp.int32, (1, T), 1)
    live = jnp.where(slots < len_ref[x], 1.0, 0.0).astype(f32)
    count = (len_ref[0] + len_ref[1] + len_ref[2] + len_ref[3]).astype(f32)
    factor = live * lax.rsqrt(total / D + 1e-05)

    gain_down = jnp.broadcast_to(gain[...], (LANE, F)).T
    for k in range(T // LANE):
        part = slice(k * LANE, (k + 1) * LANE)
        lens = gain_down * turned[:, part] * factor[:, part]
        rows[0, :, part] = lens.astype(bf16)
        cols[0, y, part, :] = lens.T.astype(bf16)

    def z_copy(hop, way):
        if hop < 4:
            src = rows.at[0 if hop == 1 else 2 * hop - 3 + way]
            dst = rows.at[2 * hop - 1 + way]
        else:
            half = pl.ds(way * (F // 2), F // 2)
            src, dst = rows.at[5 + way, half], rows.at[7, half]
        return copy(src, dst, z_sem, (2 * (hop - 1) + way,), at_z(1 - 2 * way))

    def y_copy(hop, way, block):
        ref = cols.at[0, block]
        if hop == 2:
            ref = cols.at[0, block, pl.ds(way * (T // 2), T // 2)]
        return copy(ref, ref, y_sem, (2 * (hop - 1) + way,), at_y(1 - 2 * way))

    def relay(k):
        block = (y + (0, 3, 1, 2)[k]) % NY
        return copy(cols.at[0, block], cols.at[1, block], relay_sem, (k,), other)

    def start_relay(k):
        @pl.when(c == 1)
        def _():
            relay(k).start()

    before, after, across = (y + 3) % NY, (y + 1) % NY, (y + 2) % NY

    def rows_out():
        for way in range(2):
            z_copy(1, way).start()

    for way in range(2):
        y_copy(1, way, y).start()
    start_relay(0)
    pl.when(c == 0)(rows_out)

    def rows_in(hop):
        for way in range(2):
            z_copy(hop, way).wait_recv()
            if hop < 4:
                z_copy(hop + 1, way).start()

    def columns_near():
        y_copy(1, 0, before).wait_recv()
        y_copy(2, 0, before).start()
        y_copy(1, 1, after).wait_recv()
        y_copy(2, 1, after).start()
        start_relay(1)
        start_relay(2)

    def columns_far():
        for way in range(2):
            y_copy(2, way, across).wait_recv()
        start_relay(3)

    def relayed(*ks):
        @pl.when(c == 0)
        def _():
            for k in ks:
                relay(k).wait_recv()

    def place_of(s):
        m = (s + 1) // 2
        zz = (z + NZ + jnp.where(s % 2 == 1, -m, m)) % NZ
        return zz // 2, zz % 2

    def position(dest, way):
        return jnp.where(way == 0, x + NX - dest - 1, dest + NX - 1 - x) % NX

    units = 4 - 2 * c

    def unit_of(way, j):
        r = jnp.where(c == 0, j, 2 * way + j)
        hop = jnp.where(r == 0, 0, jnp.where(r == 3, 2, jnp.where(r == 1, 3, 1)))
        return 4 * way + j, way * (1 - c), hop

    def ring_copy(s, u, way):
        return copy(sbuf.at[s, u], rbuf.at[s, u], ring_sem, (s, u), at_x(jnp.where(way == 0, 1, 3)))

    def last_rows(b, block):
        return pl.ds(pl.multiple_of(b * (NY * F) + block * F, F), F)

    def last_copy(k, b, layer, u, block):
        return copy(fin.at[b, u], out.at[layer, last_rows(b, block)], last_sem, (k, b, layer), at_y(k))

    def local_copy(b, layer, u):
        return pltpu.make_async_copy(fin.at[b, u], out.at[layer, last_rows(b, y)], local_sem.at[b, layer])

    def multiply(s, starts, way, first, last):
        def some(r, n):
            places = [unit_of(way, jnp.where(c == 0, r + k, r + k - 2 * way)) for k in range(n)]
            accs = [
                jnp.dot(rows[s], cols[layer, (y + hop) % NY], preferred_element_type=f32) for _u, layer, hop in places
            ]
            for (u, _layer, _hop), acc in zip(places, accs):
                if starts:
                    sbuf[s, u] = acc.astype(bf16)
                    ring_copy(s, u, way).start()
                else:
                    own[s, u] = acc

        def two(k, carry):
            some(first + 2 * k, 2)
            return carry

        many = jnp.maximum(last - first, 0)
        lax.fori_loop(0, many // 2, two, 0)

        @pl.when(many % 2 == 1)
        def _():
            some(last - 1, 1)

    def add(s, p, way, first, last):
        _dest, b = place_of(s)

        def one(r, carry):
            u, layer, hop = unit_of(way, jnp.where(c == 0, r, r - 2 * way))
            ring_copy(s, u, way).wait_recv()
            acc = own[s, u] + rbuf[s, u].astype(f32)
            if p < 3:
                sbuf[s, u] = acc.astype(bf16)
                ring_copy(s, u, way).start()
            else:
                fin[b, u] = (acc / count).astype(bf16)

                @pl.when(hop == 0)
                def _():
                    local_copy(b, layer, u).start()

                @pl.when(hop != 0)
                def _():
                    last_copy(hop, b, layer, u, y).start()

            return carry

        lax.fori_loop(first, last, one, 0)

    def mine(pair):
        return jnp.where(c == 0, pair[0], pair[1])

    rows_step = [mine([way[g] for way in ROWS]) for g in range(5)]
    near, far = [mine([way[k] for way in COLUMNS]) for k in range(2)]

    def columns_by(a):
        return jnp.where(a < near, 1, jnp.where(a < far, 3, 4))

    def rows_at(s):
        m = (s + 1) // 2
        at = rows_step[0]
        for g in range(1, 5):
            at = jnp.where(m == g, rows_step[g], at)
        return at

    def step(tau, carry):
        @pl.when((c == 1) & (tau == START))
        def _():
            rows_out()

        @pl.when(tau == near)
        def _():
            columns_near()
            relayed(1, 2)

        @pl.when(tau == far)
        def _():
            columns_far()
            relayed(3)

        for hop in range(1, 5):

            @pl.when(tau == rows_step[hop])
            def _(hop=hop):
                rows_in(hop)

        for turn in range(5):
            p = turn % 4
            a = tau - mine([way[p] for way in LAGS])
            before_a = sum(jnp.where(at < a, 1, 0) for at in rows_step)
            by_a = sum(jnp.where(at <= a, 1, 0) for at in rows_step)
            s_from = jnp.where((a == near) | (a == far), 0, jnp.maximum(2 * before_a - 1, 0))
            s_to = jnp.minimum(jnp.maximum(2 * by_a - 1, 0), NZ)
            upto, already = columns_by(a), columns_by(a - 1)

            def one(k, carry, turn=turn, p=p, a=a, upto=upto, already=already):
                s, way = k // 2, k % 2
                at = position(place_of(s)[0], way)

                @pl.when(at > 0 if turn == 4 else at == p)
                def _():
                    first = jnp.where(rows_at(s) == a, 0, already)
                    low, high = jnp.where(c == 0, 0, 2 * way), jnp.where(c == 0, 4, 2 * way + 2)
                    first, last = jnp.maximum(first, low), jnp.minimum(upto, high)
                    if p == 0:
                        multiply(s, turn == 0, way, first, last)
                    else:
                        add(s, p, way, first, last)

                return carry

            lax.fori_loop(2 * s_from, 2 * s_to, one, 0)
        return carry

    relayed(0)
    lax.fori_loop(0, STEPS, step, 0)

    def ending(k, carry):
        b, layer = k % 2, k // 2
        for hop in range(1, NY):
            last_copy(hop, b, layer, 0, (y + NY - hop) % NY).wait_recv()
            last_copy(hop, b, layer, 0, y).wait_send()
        local_copy(b, layer, 0).wait()
        return carry

    lax.fori_loop(0, 2 * (2 - c), ending, 0)

    def sent(k, carry):
        s, way = k // 2, k % 2
        dest, _b = place_of(s)

        @pl.when(position(dest, way) < 3)
        def _():
            def one(j, carry):
                ring_copy(s, 4 * way + j, way).wait_send()
                return carry

            lax.fori_loop(0, units, one, 0)

        return carry

    lax.fori_loop(0, 2 * NZ, sent, 0)
    for k in range(1, NZ):
        zstat_copy(k, z).wait_send()
    for k in range(1, NY):
        ystat_copy(k, y).wait_send()
    for way in range(2):
        for hop in range(1, 5):
            z_copy(hop, way).wait_send()
        y_copy(1, way, y).wait_send()
        y_copy(2, way, (before, after)[way]).wait_send()

    @pl.when(c == 0)
    def _():
        early_copy.wait_send()

    @pl.when(c == 1)
    def _():
        for k in range(4):
            relay(k).wait_send()


def products(lengths, base, delta, gain):
    f32, bf16 = jnp.float32, jnp.bfloat16
    dma = pltpu.SemaphoreType.DMA
    return pl.pallas_call(
        kernel,
        out_shape=jax.ShapeDtypeStruct((2, 2 * NY * F, F), bf16),
        in_specs=[pl.BlockSpec(memory_space=pl.ANY)] * 4,
        out_specs=pl.BlockSpec(memory_space=pl.ANY),
        scratch_shapes=[
            pltpu.SMEM((NX,), jnp.int32),
            pltpu.VMEM((T, F), bf16),
            pltpu.VMEM((T, F), bf16),
            pltpu.VMEM((1, F), f32),
            pltpu.VMEM((T, F), bf16),
            pltpu.VMEM((F, T), f32),
            pltpu.VMEM((NZ, 1, T), f32),
            pltpu.VMEM((NY, 1, T), f32),
            pltpu.VMEM((NZ, F, T), bf16),
            pltpu.VMEM((2, NY, T, F), bf16),
            pltpu.VMEM((NZ, 8, F, F), bf16),
            pltpu.VMEM((NZ, 8, F, F), bf16),
            pltpu.VMEM((2, 8, F, F), bf16),
            pltpu.VMEM((NZ, 8, F, F), f32),
            dma((2,)),
            dma((2, NZ)),
            dma((2, NY)),
            dma((2, 8)),
            dma((2, 4)),
            dma((2, 4)),
            dma((2, NZ, 8)),
            dma((2, NY, 2, 2)),
            dma((2, 2)),
            dma((4,)),
        ],
        compiler_params=pltpu.CompilerParams(
            collective_id=0, has_side_effects=True, vmem_limit_bytes=62 * 1024 * 1024
        ),
        cost_estimate=pl.CostEstimate(flops=8 * 2 * F * T * 2048, bytes_accessed=8 << 20, transcendentals=0),
    )(lengths, base, delta, gain)


def shards(base, deltas, gain, lengths):
    summed = products(lengths, base, deltas[0], gain[None, :]).astype(jnp.float32)
    gram = summed[0]
    cross = jnp.where(lax.axis_index("section") == 0, summed[1], summed[0])
    return gram[None], cross[None]


def solution(mesh):
    placed = (P("dp", "tensor"), P("section", "dp", "tensor"), P("tensor"), P())
    return jax.shard_map(
        shards,
        mesh=mesh,
        in_specs=placed,
        out_specs=(P("section", "dp", "tensor"), P("section", "dp", "tensor")),
        check_vma=False,
    )
```
